256 devices in a mesh: row: 8 (over z), col: 32 (over x, y, core).
Axes of the slice: x: 4, y: 4, z: 8, core: 2. Of those that a mesh axis runs over, the one named last changes fastest.
Arguments:
- tokens: bfloat16 [2, 2048, 4096], P(None, 'col', 'row'), may hold values from -12 to 12
- cotangent: bfloat16 [2, 2048, 4096], P(None, 'col', 'row'), may hold values from -1.5 to 1.5
- wi_gate: bfloat16 [4096, 10240], P('row', 'col'), may hold values from -1 to 1
- wi_lin: bfloat16 [4096, 10240], P('row', 'col'), may hold values from -1 to 1
- wo: bfloat16 [10240, 4096], P('col', 'row'), may hold values from -1 to 1
- rows_gate: float32 [4096], P('row'), may hold values from 0.5 to 2
- cols_gate: float32 [10240], P('col'), may hold values from 0.5 to 2
- rows_lin: float32 [4096], P('row'), may hold values from 0.5 to 2
- cols_lin: float32 [10240], P('col'), may hold values from 0.5 to 2
- rows_out: float32 [10240], P('col'), may hold values from 0.5 to 2
- cols_out: float32 [4096], P('row'), may hold values from 0.5 to 2
- rate: float32 [1], replicated, may hold values from 0.5 to 2
Outputs:
- grad_tokens: bfloat16 [2, 2048, 4096], P(None, 'col', 'row')
- update_gate: float32 [4096, 10240], P('row', 'col')
- update_lin: float32 [4096, 10240], P('row', 'col')
- update_out: float32 [10240, 4096], P('col', 'row')
- rows_gate_new: float32 [4096], P('row')
- cols_gate_new: float32 [10240], P('col')
- rows_lin_new: float32 [4096], P('row')
- cols_lin_new: float32 [10240], P('col')
- rows_out_new: float32 [10240], P('col')
- cols_out_new: float32 [4096], P('row')
The draws below stay inside these ranges and needn't reach their ends.
All inputs are finite; a program needn't handle non-finite values.
Results may differ from the reference program's by a relative error of at most 0.034.
Values may be sent and summed in bfloat16 or wider, within the bound.
No kernel may reach another device: no remote copies, remote signals or barrier semaphores. Data moves between devices by JAX's collectives and lax.ppermute only.
A program may use at most 128 MiB of HBM per device.

```python
import math
import jax
import jax.numpy as jnp
from jax import lax

D = 4096
FF = 10240
MICRO = 2
TOK_MB = 2048
N_ROW = 8
N_COL = 32


def band_index(count):
    return jnp.arange(count, dtype=jnp.int32) * 8 // count


def hidden_targets(key):
    return jax.random.randint(jax.random.fold_in(key, 101), (8,), 0, 8)


def token_bands(key):
    return jax.random.randint(jax.random.fold_in(key, 102), (MICRO, TOK_MB), 0, 8)


def banded_weight(base, match, fan):
    strong = math.sqrt(0.9 * 8.0 / fan)
    faint = math.sqrt(0.1 * 8.0 / (7.0 * fan))
    return (jnp.clip(base, -2.9, 2.9) * jnp.where(match, strong, faint)).astype(jnp.bfloat16)


def weight_base(key, shape):
    first = jax.random.fold_in(key, 0)
    normal_part = jax.random.normal(first, shape, jnp.float32)
    return normal_part


def draw_wi_gate(key, part):
    targets = hidden_targets(key)
    key = jax.random.fold_in(key, 21)
    match = band_index(D)[:, None] == targets[band_index(FF)][None, :]
    return banded_weight(weight_base(key, (D, FF)), match, D)


def draw_wi_lin(key, part):
    targets = hidden_targets(key)
    key = jax.random.fold_in(key, 22)
    match = band_index(D)[:, None] == targets[band_index(FF)][None, :]
    return banded_weight(weight_base(key, (D, FF)), match, D)


def draw_wo(key, part):
    targets = hidden_targets(key)
    key = jax.random.fold_in(key, 23)
    match = targets[band_index(FF)][:, None] == band_index(D)[None, :]
    return banded_weight(weight_base(key, (FF, D)), match, FF)


def banded_rows(key, base, types, level):
    jitter = jax.random.uniform(key, (D,), jnp.float32, 0.8, 1.1)
    loud = types[:, :, None] == band_index(D)[None, None, :]
    scales = jnp.where(loud, 3.6 * level, 0.9 * level) * jitter[None, None, :]
    return (jnp.clip(base, -3.0, 3.0) * scales).astype(jnp.bfloat16)


def draw_tokens(key, part):
    types = token_bands(key)
    key = jax.random.fold_in(key, 11)
    first, second = jax.random.split(key, 2)
    base = jax.random.normal(second, (MICRO, TOK_MB, D), jnp.float32)
    return banded_rows(first, base, types, 1.0)


def draw_cotangent(key, part):
    types = token_bands(key)
    key = jax.random.fold_in(key, 12)
    first, second = jax.random.split(key, 2)
    base = jax.random.normal(second, (MICRO, TOK_MB, D), jnp.float32)
    return banded_rows(first, base, types, 0.12)


def banded_state(key, count):
    first, second = jax.random.split(key)
    draw = jax.random.uniform(first, (8,), jnp.float32)
    level = draw
    logs = math.log(0.56) + (math.log(1.8) - math.log(0.56)) * level
    jitter = jax.random.uniform(second, (count,), jnp.float32, math.log(0.9), math.log(1.1))
    return jnp.exp(logs[band_index(count)] + jitter)


def draw_rows_gate(key, part):
    key = jax.random.fold_in(key, 31)
    return banded_state(key, D)


def draw_cols_gate(key, part):
    key = jax.random.fold_in(key, 32)
    return banded_state(key, FF)


def draw_rows_lin(key, part):
    key = jax.random.fold_in(key, 33)
    return banded_state(key, D)


def draw_cols_lin(key, part):
    key = jax.random.fold_in(key, 34)
    return banded_state(key, FF)


def draw_rows_out(key, part):
    key = jax.random.fold_in(key, 35)
    return banded_state(key, FF)


def draw_cols_out(key, part):
    key = jax.random.fold_in(key, 36)
    return banded_state(key, D)


def setup_inputs(seed: int = 0) -> dict:
    key_of = jax.random.split(jax.random.key(seed), 13)
    tokens = draw_tokens(jax.random.fold_in(key_of[12], 71), 0)
    cotangent = draw_cotangent(jax.random.fold_in(key_of[12], 71), 0)
    wi_gate = draw_wi_gate(jax.random.fold_in(key_of[12], 71), 0)
    wi_lin = draw_wi_lin(jax.random.fold_in(key_of[12], 71), 0)
    wo = draw_wo(jax.random.fold_in(key_of[12], 71), 0)
    rows_gate = draw_rows_gate(jax.random.fold_in(key_of[12], 71), 0)
    cols_gate = draw_cols_gate(jax.random.fold_in(key_of[12], 71), 0)
    rows_lin = draw_rows_lin(jax.random.fold_in(key_of[12], 71), 0)
    cols_lin = draw_cols_lin(jax.random.fold_in(key_of[12], 71), 0)
    rows_out = draw_rows_out(jax.random.fold_in(key_of[12], 71), 0)
    cols_out = draw_cols_out(jax.random.fold_in(key_of[12], 71), 0)
    rate = jnp.clip(jnp.exp(jax.random.uniform(key_of[11], (1,), jnp.float32, math.log(0.5), math.log(2.0))), 0.5, 2.0)
    return {"tokens": tokens, "cotangent": cotangent, "wi_gate": wi_gate, "wi_lin": wi_lin, "wo": wo, "rows_gate": rows_gate, "cols_gate": cols_gate, "rows_lin": rows_lin, "cols_lin": cols_lin, "rows_out": rows_out, "cols_out": cols_out, "rate": rate}


decay_rate = 0.8
gelu_coeff = math.sqrt(2.0 / math.pi)

def gelu_parts(value):
    inner = gelu_coeff * (value + 0.044715 * value * value * value)
    tangent = jnp.tanh(inner)
    gelu_value = 0.5 * value * (1.0 + tangent)
    gelu_slope = 0.5 * (1.0 + tangent) + 0.5 * value * (1.0 - tangent * tangent) * gelu_coeff * (1.0 + 3.0 * 0.044715 * value * value)
    return (gelu_value, gelu_slope)

def blocked_product(left, right):
    block = left.shape[1] // N_ROW
    total = jnp.zeros((left.shape[0], right.shape[1]), jnp.float32)
    for block_index in range(N_ROW):
        low = block_index * block
        partial_term = jnp.dot(left[:, low:low + block], right[low:low + block, :], preferred_element_type=jnp.float32)
        rounded = lax.optimization_barrier(partial_term.astype(jnp.bfloat16))
        total = total + rounded.astype(jnp.float32)
    return total

def hidden_blocked(grad_gate_pre, grad_lin_pre, wi_gate, wi_lin):
    block = FF // N_COL
    total = jnp.zeros((grad_gate_pre.shape[0], D), jnp.float32)
    for block_index in range(N_COL):
        low = block_index * block
        partial_term = jnp.dot(grad_gate_pre[:, low:low + block], wi_gate[:, low:low + block].T, preferred_element_type=jnp.float32)
        partial_term = partial_term + jnp.dot(grad_lin_pre[:, low:low + block], wi_lin[:, low:low + block].T, preferred_element_type=jnp.float32)
        rounded = lax.optimization_barrier(partial_term.astype(jnp.bfloat16))
        total = total + rounded.astype(jnp.float32)
    return total

def adafactor(grad, rows_old, cols_old, rate):
    squares = grad * grad + 1e-30
    rows_new = decay_rate * rows_old + (1.0 - decay_rate) * lax.optimization_barrier(jnp.sum(squares, 1)) / squares.shape[1]
    cols_new = decay_rate * cols_old + (1.0 - decay_rate) * lax.optimization_barrier(jnp.sum(squares, 0)) / squares.shape[0]
    unit = grad / jnp.sqrt(rows_new[:, None] * cols_new[None, :])
    rms = jnp.sqrt(jnp.sum(unit * unit) / (unit.shape[0] * unit.shape[1]) + 1e-06)
    return (-rate[0] * unit / rms, rows_new, cols_new)

def reference(tokens, cotangent, wi_gate, wi_lin, wo, rows_gate, cols_gate, rows_lin, cols_lin, rows_out, cols_out, rate):
    grad_gate = jnp.zeros((D, FF), jnp.float32)
    grad_lin = jnp.zeros((D, FF), jnp.float32)
    grad_out = jnp.zeros((FF, D), jnp.float32)
    results = []
    for micro_index in range(MICRO):
        inputs = tokens[micro_index]
        upstream = cotangent[micro_index]
        pre_gate = blocked_product(inputs, wi_gate)
        pre_lin = blocked_product(inputs, wi_lin)
        grad_act = blocked_product(upstream, wo.T)
        gelu_value, gelu_slope = gelu_parts(pre_gate)
        act = (gelu_value * pre_lin).astype(jnp.bfloat16)
        grad_gate_pre = (grad_act * pre_lin * gelu_slope).astype(jnp.bfloat16)
        grad_lin_pre = (grad_act * gelu_value).astype(jnp.bfloat16)
        grad_gate = grad_gate + jnp.dot(inputs.T, grad_gate_pre, preferred_element_type=jnp.float32)
        grad_lin = grad_lin + jnp.dot(inputs.T, grad_lin_pre, preferred_element_type=jnp.float32)
        grad_out = grad_out + jnp.dot(act.T, upstream, preferred_element_type=jnp.float32)
        grad_in = hidden_blocked(grad_gate_pre, grad_lin_pre, wi_gate, wi_lin)
        results.append(grad_in.astype(jnp.bfloat16))
    scale = 1.0 / math.sqrt(MICRO * TOK_MB)
    update_gate, rows_gate_new, cols_gate_new = adafactor(grad_gate * scale, rows_gate, cols_gate, rate)
    update_lin, rows_lin_new, cols_lin_new = adafactor(grad_lin * scale, rows_lin, cols_lin, rate)
    update_out, rows_out_new, cols_out_new = adafactor(grad_out * scale, rows_out, cols_out, rate)
    return (jnp.stack(results, 0), update_gate, update_lin, update_out, rows_gate_new, cols_gate_new, rows_lin_new, cols_lin_new, rows_out_new, cols_out_new)
```

```python
import math

import jax
import jax.numpy as jnp
from jax import lax
from jax.experimental import pallas as pl
from jax.experimental.pallas import tpu as pltpu
from jax.sharding import Mesh
from jax.sharding import PartitionSpec as P

D = 4096
FF = 10240
NZ, NX, NY, NC = 8, 4, 4, 2
TOK = 512
GRP = 128
DB = D // NZ
FB = FF // (NX * NY * NC)

decay_rate = 0.8
gelu_coeff = math.sqrt(2.0 / math.pi)
COL = ("x", "y", "c")
ALL = ("z", "x", "y", "c")
VMEM = 48 * 1024 * 1024


def device(z, x, y, c):
    return ((z * NX + x) * NY + y) * NC + c


def token_moves():
    moves = []
    for z in range(NZ):
        for x in range(NX):
            for y in range(NY):
                for c in range(NC):
                    target = device(2 * x + c, (z // 2 + x) % NX, y, z % 2)
                    moves.append((device(z, x, y, c), target))
    return moves


MOVES = token_moves()
BACK = [(target, source) for source, target in MOVES]


def shifted(value, axis, step):
    return lax.ppermute(value, axis, [((i + step) % 4, i) for i in range(4)])


def partner(value, axis, size, bits):
    return lax.ppermute(value, axis, [(i, i ^ bits) for i in range(size)])


def swap(value):
    return partner(value, "c", 2, 1)


def gather4(value, axis):
    return jnp.stack([value] + [shifted(value, axis, step) for step in (1, 2, 3)], 0)


def sum4(value, axis):
    a = [value] + [partner(value, axis, 4, bits) for bits in (1, 2, 3)]
    return (a[0] + a[1]) + (a[2] + a[3])


def sum_col(value):
    value = value + swap(value)
    return sum4(sum4(value, "x"), "y")


def sum_z(value):
    a = [value] + [partner(value, "z", 8, bits) for bits in range(1, 8)]
    return ((a[0] + a[1]) + (a[2] + a[3])) + ((a[4] + a[5]) + (a[6] + a[7]))


def gelu_parts(value):
    inner = gelu_coeff * (value + 0.044715 * value * value * value)
    tangent = jnp.tanh(inner)
    gelu_value = 0.5 * value * (1.0 + tangent)
    gelu_slope = 0.5 * (1.0 + tangent) + 0.5 * value * (1.0 - tangent * tangent) * gelu_coeff * (
        1.0 + 3.0 * 0.044715 * value * value
    )
    return (gelu_value, gelu_slope)


def dot_nt(left, right):
    return lax.dot_general(
        left, right, (((1,), (1,)), ((), ())), preferred_element_type=jnp.float32
    )


def forward_kernel(order, tok0, tok1, cot0, cot1, weight, hidden_t, hidden, acc):
    i = pl.program_id(0)

    @pl.when(i == 0)
    def _():
        acc[...] = jnp.zeros_like(acc)

    def add(tok, cot):
        acc[: 2 * FB] += dot_nt(weight[0, : 2 * FB], tok[...].reshape(TOK, DB))
        acc[2 * FB :] += dot_nt(weight[0, 2 * FB :], cot[...].reshape(TOK, DB))

    @pl.when(i < 4)
    def _():
        add(tok0, cot0)

    @pl.when(i >= 4)
    def _():
        add(tok1, cot1)

    @pl.when(i == NZ - 1)
    def _():
        pre_gate = acc[:FB]
        pre_lin = acc[FB : 2 * FB]
        grad_act = acc[2 * FB :]
        gelu_value, gelu_slope = gelu_parts(pre_gate)
        gate = grad_act * pre_lin * gelu_slope
        lin = grad_act * gelu_value
        hidden_t[:FB] = gate.astype(jnp.bfloat16)
        hidden_t[FB : 2 * FB] = lin.astype(jnp.bfloat16)
        hidden_t[2 * FB :] = (gelu_value * pre_lin).astype(jnp.bfloat16)
        hidden[...] = hidden_t[: 2 * FB].T


def weight_grad_kernel(order, tok0, tok1, cot0, cot1, hidden_t, grad):
    i = pl.program_id(0)

    def emit(tok, cot):
        grad[0, : 2 * FB] = jnp.dot(
            hidden_t[: 2 * FB], tok[...].reshape(TOK, DB), preferred_element_type=jnp.float32
        ).astype(jnp.bfloat16)
        grad[0, 2 * FB :] = jnp.dot(
            hidden_t[2 * FB :], cot[...].reshape(TOK, DB), preferred_element_type=jnp.float32
        ).astype(jnp.bfloat16)

    @pl.when(i < 4)
    def _():
        emit(tok0, cot0)

    @pl.when(i >= 4)
    def _():
        emit(tok1, cot1)


def token_grad_kernel(order, hidden, weight, grad):
    product = jnp.dot(hidden[...], weight[0], preferred_element_type=jnp.float32)
    product = product.astype(jnp.bfloat16)
    for shift in range(4):
        grad[0, 0, order[12 + shift]] = product[shift * GRP : (shift + 1) * GRP]


def block_specs():
    tok0 = pl.BlockSpec((4, 1, GRP, DB), lambda i, o: (0, jnp.minimum(i, 3), 0, 0))
    tok1 = pl.BlockSpec((4, 1, GRP, DB), lambda i, o: (0, jnp.maximum(i - 4, 0), 0, 0))
    cot0 = pl.BlockSpec((1, 4, GRP, DB), lambda i, o: (jnp.minimum(i, 3), 0, 0, 0))
    cot1 = pl.BlockSpec((1, 4, GRP, DB), lambda i, o: (jnp.maximum(i - 4, 0), 0, 0, 0))
    return [tok0, tok1, cot0, cot1]


def forward(order, blocks, weight):
    return pl.pallas_call(
        forward_kernel,
        grid_spec=pltpu.PrefetchScalarGridSpec(
            num_scalar_prefetch=1,
            grid=(NZ,),
            in_specs=block_specs() + [pl.BlockSpec((1, 3 * FB, DB), lambda i, o: (o[i], 0, 0))],
            out_specs=[
                pl.BlockSpec((3 * FB, TOK), lambda i, o: (0, 0)),
                pl.BlockSpec((TOK, 2 * FB), lambda i, o: (0, 0)),
            ],
            scratch_shapes=[pltpu.VMEM((3 * FB, TOK), jnp.float32)],
        ),
        out_shape=[
            jax.ShapeDtypeStruct((3 * FB, TOK), jnp.bfloat16),
            jax.ShapeDtypeStruct((TOK, 2 * FB), jnp.bfloat16),
        ],
        compiler_params=pltpu.CompilerParams(vmem_limit_bytes=VMEM),
        cost_estimate=pl.CostEstimate(
            flops=2 * 3 * FB * TOK * D, bytes_accessed=17000000, transcendentals=FB * TOK
        ),
    )(order, *blocks, weight)


def weight_grad(order, blocks, hidden_t):
    return pl.pallas_call(
        weight_grad_kernel,
        grid_spec=pltpu.PrefetchScalarGridSpec(
            num_scalar_prefetch=1,
            grid=(NZ,),
            in_specs=block_specs() + [pl.BlockSpec((3 * FB, TOK), lambda i, o: (0, 0))],
            out_specs=pl.BlockSpec((1, 3 * FB, DB), lambda i, o: (o[i], 0, 0)),
        ),
        out_shape=jax.ShapeDtypeStruct((NZ, 3 * FB, DB), jnp.bfloat16),
        compiler_params=pltpu.CompilerParams(vmem_limit_bytes=VMEM),
        cost_estimate=pl.CostEstimate(
            flops=2 * 3 * FB * TOK * D, bytes_accessed=17000000, transcendentals=0
        ),
    )(order, *blocks, hidden_t)


def token_grad(order, hidden, weight):
    return pl.pallas_call(
        token_grad_kernel,
        grid_spec=pltpu.PrefetchScalarGridSpec(
            num_scalar_prefetch=1,
            grid=(NZ,),
            in_specs=[
                pl.BlockSpec((TOK, 2 * FB), lambda i, o: (0, 0)),
                pl.BlockSpec((1, 2 * FB, DB), lambda i, o: (o[i], 0, 0)),
            ],
            out_specs=pl.BlockSpec((1, 1, 4, GRP, DB), lambda i, o: (i // 4, o[8 + i % 4], 0, 0, 0)),
        ),
        out_shape=jax.ShapeDtypeStruct((2, 4, 4, GRP, DB), jnp.bfloat16),
        compiler_params=pltpu.CompilerParams(vmem_limit_bytes=VMEM),
        cost_estimate=pl.CostEstimate(
            flops=2 * 2 * FB * TOK * D, bytes_accessed=10000000, transcendentals=0
        ),
    )(order, hidden, weight)


def local(
    tokens,
    cotangent,
    wi_gate,
    wi_lin,
    wo,
    rows_gate,
    cols_gate,
    rows_lin,
    cols_lin,
    rows_out,
    cols_out,
    rate,
):
    bf16 = jnp.bfloat16
    z, x, y, c = (lax.axis_index(axis) for axis in ALL)
    weight = lax.all_gather(jnp.concatenate([wi_gate.T, wi_lin.T, wo], 0), "z", axis=0)

    pair = jnp.stack([tokens.reshape(GRP, DB), cotangent.reshape(GRP, DB)], 0)
    pair = lax.ppermute(pair, ALL, MOVES)
    tok0 = gather4(gather4(pair[0], "x"), "y")
    cot0 = gather4(gather4(pair[1], "y"), "x")
    blocks = [tok0, swap(tok0), cot0, swap(cot0)]
    shift = jnp.arange(4, dtype=jnp.int32)
    high = (x + shift - z // 2 + NX) % NX
    order = jnp.concatenate(
        [2 * high + c, 2 * high + (1 - c), (x + shift) % NX, (y + shift) % NY]
    ).astype(jnp.int32)

    hidden_t, hidden = forward(order, blocks, weight)
    grad_w = lax.psum_scatter(weight_grad(order, blocks, hidden_t), "z", scatter_dimension=0)

    part = token_grad(order, hidden, weight)
    part = (part[0].astype(jnp.float32) + swap(part[1]).astype(jnp.float32)).astype(bf16)
    part = part.reshape(NX * NY, GRP, DB)
    part = lax.all_to_all(part, ("x", "y"), 0, 0, tiled=True)
    part = jnp.sum(part.astype(jnp.float32), 0).astype(bf16)
    grad_tokens = lax.ppermute(part, ALL, BACK).reshape(tokens.shape)

    grad = grad_w.astype(jnp.float32) * (1.0 / math.sqrt(4096.0))
    keep = 1.0 - decay_rate
    squares = grad * grad + 1e-30
    over_model = sum_z(jnp.sum(squares, 1))
    hidden_old = jnp.concatenate([cols_gate, cols_lin, rows_out])
    hidden_new = decay_rate * hidden_old + keep * over_model / D
    model_old = jnp.stack([rows_gate, rows_lin, cols_out], 0)
    weighted = grad * grad / hidden_new[:, None]
    over_hidden = sum_col(
        jnp.concatenate(
            [
                jnp.sum(squares.reshape(3, FB, DB), 1),
                jnp.sum(weighted.reshape(3, FB, DB), 1),
            ],
            0,
        )
    )
    model_new = decay_rate * model_old + keep * over_hidden[:3] / FF
    totals = sum_z(jnp.sum(over_hidden[3:] / model_new, 1, keepdims=True))
    factor = -rate[0] / jnp.sqrt(totals / (D * FF) + 1e-06)
    update = (
        grad.reshape(3, FB, DB)
        * lax.rsqrt(hidden_new).reshape(3, FB, 1)
        * (factor * lax.rsqrt(model_new)).reshape(3, 1, DB)
    )
    return (
        grad_tokens,
        update[0].T,
        update[1].T,
        update[2],
        model_new[0],
        hidden_new[:FB],
        model_new[1],
        hidden_new[FB : 2 * FB],
        hidden_new[2 * FB :],
        model_new[2],
    )


def solution(mesh):
    fine = Mesh(mesh.devices.reshape(NZ, NX, NY, NC), ALL)
    return jax.shard_map(
        local,
        mesh=fine,
        in_specs=(
            P(None, COL, "z"),
            P(None, COL, "z"),
            P("z", COL),
            P("z", COL),
            P(COL, "z"),
            P("z"),
            P(COL),
            P("z"),
            P(COL),
            P(COL),
            P("z"),
            P(),
        ),
        out_specs=(
            P(None, COL, "z"),
            P("z", COL),
            P("z", COL),
            P(COL, "z"),
            P("z"),
            P(COL),
            P("z"),
            P(COL),
            P(COL),
            P("z"),
        ),
        check_vma=False,
    )
```

```python
import math

import jax
import jax.numpy as jnp
from jax import lax
from jax.experimental import pallas as pl
from jax.experimental.pallas import tpu as pltpu
from jax.sharding import Mesh
from jax.sharding import PartitionSpec as P

D = 4096
FF = 10240
NZ, NX, NY, NC = 8, 4, 4, 2
TOK = 512
SUB = 16
DB = D // NZ
FB = FF // (NX * NY * NC)

decay_rate = 0.8
gelu_coeff = math.sqrt(2.0 / math.pi)
COL = ("x", "y", "c")
VMEM = 48 * 1024 * 1024


def shifted(value, axis, step):
    return lax.ppermute(value, axis, [((i + step) % 4, i) for i in range(4)])


def swap(value):
    return lax.ppermute(value, "c", [(0, 1), (1, 0)])


def gather4(value, axis, model_dim, new_dim):
    right = shifted(value, axis, 1)
    left = shifted(value, axis, 3)
    low = lax.slice_in_dim(right, 0, NZ // 2, axis=model_dim)
    high = lax.slice_in_dim(left, NZ // 2, NZ, axis=model_dim)
    far = jnp.concatenate([shifted(low, axis, 1), shifted(high, axis, 3)], model_dim)
    return jnp.stack([value, right, far, left], new_dim)


def sum_over(value, axis, size):
    copies = jnp.broadcast_to(value[None], (size,) + value.shape)
    return jnp.sum(lax.all_to_all(copies, axis, 0, 0, tiled=True), 0)


def sum_col(value):
    return sum_over(value + swap(value), ("x", "y"), NX * NY)


def gelu_parts(value):
    inner = gelu_coeff * (value + 0.044715 * value * value * value)
    tangent = jnp.tanh(inner)
    gelu_value = 0.5 * value * (1.0 + tangent)
    gelu_slope = 0.5 * (1.0 + tangent) + 0.5 * value * (1.0 - tangent * tangent) * gelu_coeff * (
        1.0 + 3.0 * 0.044715 * value * value
    )
    return (gelu_value, gelu_slope)


def dot_nt(left, right):
    return lax.dot_general(
        left, right, (((1,), (1,)), ((), ())), preferred_element_type=jnp.float32
    )


def rows_of(own, other, k):
    return jnp.concatenate(
        [own[:, :, k].reshape(TOK // 2, DB), other[:, :, k].reshape(TOK // 2, DB)], 0
    )


def forward_kernel(tok0, tok1, cot0, cot1, weight, hidden_t, hidden, acc):
    i = pl.program_id(0)

    def products():
        first = second = 0.0
        for k in range(2):
            first += dot_nt(weight[k, : 2 * FB], rows_of(tok0, tok1, k))
            second += dot_nt(weight[k, 2 * FB :], rows_of(cot0, cot1, k))
        return first, second

    @pl.when(i == 0)
    def _():
        first, second = products()
        acc[: 2 * FB] = first
        acc[2 * FB :] = second

    @pl.when(i > 0)
    def _():
        first, second = products()
        acc[: 2 * FB] += first
        acc[2 * FB :] += second

    @pl.when(i == NZ // 2 - 1)
    def _():
        pre_gate = acc[:FB]
        pre_lin = acc[FB : 2 * FB]
        grad_act = acc[2 * FB :]
        gelu_value, gelu_slope = gelu_parts(pre_gate)
        gate = grad_act * pre_lin * gelu_slope
        lin = grad_act * gelu_value
        hidden_t[:FB] = gate.astype(jnp.bfloat16)
        hidden_t[FB : 2 * FB] = lin.astype(jnp.bfloat16)
        hidden_t[2 * FB :] = (gelu_value * pre_lin).astype(jnp.bfloat16)
        hidden[...] = hidden_t[: 2 * FB].T


def weight_grad_kernel(tok0, tok1, cot0, cot1, hidden_t, grad):
    for k in range(2):
        grad[k, : 2 * FB] = jnp.dot(
            hidden_t[: 2 * FB], rows_of(tok0, tok1, k), preferred_element_type=jnp.float32
        ).astype(jnp.bfloat16)
        grad[k, 2 * FB :] = jnp.dot(
            hidden_t[2 * FB :], rows_of(cot0, cot1, k), preferred_element_type=jnp.float32
        ).astype(jnp.bfloat16)


def token_grad_kernel(place, hidden, weight, grad):
    for k in range(2):
        product = jnp.dot(hidden[...], weight[k], preferred_element_type=jnp.float32)
        product = product.astype(jnp.bfloat16).reshape(2, NY, NX, SUB, DB)
        for y in range(NY):
            for x in range(NX):
                for core in range(2):
                    grad[core, place[y * NX + x], k] = product[core, y, x]


def block_specs():
    return [pl.BlockSpec((NY, NX, 2, SUB, DB), lambda i: (0, 0, i, 0, 0))] * 4


def forward(blocks, weight):
    return pl.pallas_call(
        forward_kernel,
        grid=(NZ // 2,),
        in_specs=block_specs() + [pl.BlockSpec((2, 3 * FB, DB), lambda i: (i, 0, 0))],
        out_specs=[
            pl.BlockSpec((3 * FB, TOK), lambda i: (0, 0)),
            pl.BlockSpec((TOK, 2 * FB), lambda i: (0, 0)),
        ],
        scratch_shapes=[pltpu.VMEM((3 * FB, TOK), jnp.float32)],
        out_shape=[
            jax.ShapeDtypeStruct((3 * FB, TOK), jnp.bfloat16),
            jax.ShapeDtypeStruct((TOK, 2 * FB), jnp.bfloat16),
        ],
        compiler_params=pltpu.CompilerParams(vmem_limit_bytes=VMEM),
        cost_estimate=pl.CostEstimate(
            flops=2 * 3 * FB * TOK * D, bytes_accessed=17000000, transcendentals=FB * TOK
        ),
    )(*blocks, weight)


def weight_grad(blocks, hidden_t):
    return pl.pallas_call(
        weight_grad_kernel,
        grid=(NZ // 2,),
        in_specs=block_specs() + [pl.BlockSpec((3 * FB, TOK), lambda i: (0, 0))],
        out_specs=pl.BlockSpec((2, 3 * FB, DB), lambda i: (i, 0, 0)),
        out_shape=jax.ShapeDtypeStruct((NZ, 3 * FB, DB), jnp.bfloat16),
        compiler_params=pltpu.CompilerParams(vmem_limit_bytes=VMEM),
        cost_estimate=pl.CostEstimate(
            flops=2 * 3 * FB * TOK * D, bytes_accessed=17000000, transcendentals=0
        ),
    )(*blocks, hidden_t)


def token_grad(place, hidden, weight):
    return pl.pallas_call(
        token_grad_kernel,
        grid_spec=pltpu.PrefetchScalarGridSpec(
            num_scalar_prefetch=1,
            grid=(NZ // 2,),
            in_specs=[
                pl.BlockSpec((TOK, 2 * FB), lambda i, p: (0, 0)),
                pl.BlockSpec((2, 2 * FB, DB), lambda i, p: (i, 0, 0)),
            ],
            out_specs=pl.BlockSpec((2, NX * NY, 2, SUB, DB), lambda i, p: (0, 0, i, 0, 0)),
        ),
        out_shape=jax.ShapeDtypeStruct((2, NX * NY, NZ, SUB, DB), jnp.bfloat16),
        compiler_params=pltpu.CompilerParams(vmem_limit_bytes=VMEM),
        cost_estimate=pl.CostEstimate(
            flops=2 * 2 * FB * TOK * D, bytes_accessed=10000000, transcendentals=0
        ),
    )(place, hidden, weight)


def local(
    tokens,
    cotangent,
    wi_gate,
    wi_lin,
    wo,
    rows_gate,
    cols_gate,
    rows_lin,
    cols_lin,
    rows_out,
    cols_out,
    rate,
):
    bf16 = jnp.bfloat16
    weight = lax.all_gather(jnp.concatenate([wi_gate.T, wi_lin.T, wo], 0), "z", axis=0)

    pair = jnp.stack([tokens.reshape(NZ, SUB, DB), cotangent.reshape(NZ, SUB, DB)], 1)
    pair = lax.all_to_all(pair, "z", 0, 0, tiled=True)
    tok = gather4(gather4(pair[:, 0], "x", 0, 0), "y", 1, 0)
    cot = gather4(gather4(pair[:, 1], "y", 0, 0), "x", 1, 1)
    blocks = [tok, swap(tok), cot, swap(cot)]

    hidden_t, hidden = forward(blocks, weight)
    grad_w = lax.psum_scatter(weight_grad(blocks, hidden_t), "z", scatter_dimension=0)

    shift = jnp.arange(4, dtype=jnp.int32)
    x_of = (lax.axis_index("x") + shift) % NX
    y_of = (lax.axis_index("y") + shift) % NY
    place = (x_of[None, :] * NY + y_of[:, None]).astype(jnp.int32).reshape(NX * NY)
    part = token_grad(place, hidden, weight)
    part = (part[0].astype(jnp.float32) + swap(part[1]).astype(jnp.float32)).astype(bf16)
    part = lax.all_to_all(part, ("x", "y"), 0, 0, tiled=True)
    part = jnp.sum(part.astype(jnp.float32), 0).astype(bf16)
    grad_tokens = lax.all_to_all(part, "z", 0, 0, tiled=True).reshape(tokens.shape)
    grad_w, grad_tokens = lax.optimization_barrier((grad_w, grad_tokens))

    grad = grad_w.astype(jnp.float32) * (1.0 / math.sqrt(4096.0))
    keep = 1.0 - decay_rate
    squares = grad * grad + 1e-30
    over_model = sum_over(jnp.sum(squares, 1), "z", NZ)
    hidden_old = jnp.concatenate([cols_gate, cols_lin, rows_out])
    hidden_new = decay_rate * hidden_old + keep * over_model / D
    model_old = jnp.stack([rows_gate, rows_lin, cols_out], 0)
    weighted = grad * grad / hidden_new[:, None]
    over_hidden = sum_col(
        jnp.concatenate(
            [
                jnp.sum(squares.reshape(3, FB, DB), 1),
                jnp.sum(weighted.reshape(3, FB, DB), 1),
            ],
            0,
        )
    )
    model_new = decay_rate * model_old + keep * over_hidden[:3] / FF
    totals = sum_over(jnp.sum(over_hidden[3:] / model_new, 1, keepdims=True), "z", NZ)
    factor = -rate[0] / jnp.sqrt(totals / (D * FF) + 1e-06)
    update = (
        grad.reshape(3, FB, DB)
        * lax.rsqrt(hidden_new).reshape(3, FB, 1)
        * (factor * lax.rsqrt(model_new)).reshape(3, 1, DB)
    )
    return (
        grad_tokens,
        update[0].T,
        update[1].T,
        update[2],
        model_new[0],
        hidden_new[:FB],
        model_new[1],
        hidden_new[FB : 2 * FB],
        hidden_new[2 * FB :],
        model_new[2],
    )


def solution(mesh):
    fine = Mesh(mesh.devices.reshape(NZ, NX, NY, NC), ("z",) + COL)
    return jax.shard_map(
        local,
        mesh=fine,
        in_specs=(
            P(None, COL, "z"),
            P(None, COL, "z"),
            P("z", COL),
            P("z", COL),
            P(COL, "z"),
            P("z"),
            P(COL),
            P("z"),
            P(COL),
            P(COL),
            P("z"),
            P(),
        ),
        out_specs=(
            P(None, COL, "z"),
            P("z", COL),
            P("z", COL),
            P(COL, "z"),
            P("z"),
            P(COL),
            P("z"),
            P(COL),
            P(COL),
            P("z"),
        ),
        check_vma=False,
    )
```

```python
import math

import jax
import jax.numpy as jnp
from jax import lax
from jax.experimental import pallas as pl
from jax.experimental.pallas import tpu as pltpu
from jax.sharding import Mesh
from jax.sharding import PartitionSpec as P

D = 4096
FF = 10240
NZ, NX, NY, NC = 8, 4, 4, 2
TOK = 512
SUB = 16
DB = D // NZ
FB = FF // (NX * NY * NC)

decay_rate = 0.8
gelu_coeff = math.sqrt(2.0 / math.pi)
COL = ("x", "y", "c")
VMEM = 48 * 1024 * 1024


def shifted(value, axis, step):
    return lax.ppermute(value, axis, [((i + step) % 4, i) for i in range(4)])


def swap(value):
    return lax.ppermute(value, "c", [(0, 1), (1, 0)])


def gather4(value, axis, model_dim, new_dim):
    right = shifted(value, axis, 1)
    left = shifted(value, axis, 3)
    low = lax.slice_in_dim(right, 0, NZ // 2, axis=model_dim)
    high = lax.slice_in_dim(left, NZ // 2, NZ, axis=model_dim)
    far = jnp.concatenate([shifted(low, axis, 1), shifted(high, axis, 3)], model_dim)
    return jnp.stack([value, right, far, left], new_dim)


def sum_over(value, axis, size):
    copies = jnp.broadcast_to(value[None], (size,) + value.shape)
    return jnp.sum(lax.all_to_all(copies, axis, 0, 0, tiled=True), 0)


def sum_col(value):
    return sum_over(value + swap(value), ("x", "y"), NX * NY)


def gelu_parts(value):
    inner = gelu_coeff * (value + 0.044715 * value * value * value)
    tangent = jnp.tanh(inner)
    gelu_value = 0.5 * value * (1.0 + tangent)
    gelu_slope = 0.5 * (1.0 + tangent) + 0.5 * value * (1.0 - tangent * tangent) * gelu_coeff * (
        1.0 + 3.0 * 0.044715 * value * value
    )
    return (gelu_value, gelu_slope)


def dot_nt(left, right):
    return lax.dot_general(
        left, right, (((1,), (1,)), ((), ())), preferred_element_type=jnp.float32
    )


def main_kernel(tok0, tok1, cot0, cot1, weight, grad, hidden, x, w, acc, hidden_t, sems, out_sems):
    def loads(k):
        sources = (tok0, tok1, cot0, cot1)
        copies = [
            pltpu.make_async_copy(source.at[:, :, k], x.at[m // 2, k, m % 2], sems.at[k, m])
            for m, source in enumerate(sources)
        ]
        return copies + [pltpu.make_async_copy(weight.at[k], w.at[k], sems.at[k, 4])]

    def store(k):
        return pltpu.make_async_copy(w.at[k], grad.at[k], out_sems.at[k])

    def start(k, carry):
        for copy in loads(k):
            copy.start()
        return carry

    lax.fori_loop(0, NZ, start, 0)
    acc[...] = jnp.zeros_like(acc)

    def forward(pair, carry):
        first = second = 0.0
        for k in (2 * pair, 2 * pair + 1):
            for copy in loads(k):
                copy.wait()
            first += dot_nt(w[k, : 2 * FB], x[0, k].reshape(TOK, DB))
            second += dot_nt(w[k, 2 * FB :], x[1, k].reshape(TOK, DB))
        acc[: 2 * FB] += first
        acc[2 * FB :] += second
        return carry

    lax.fori_loop(0, NZ // 2, forward, 0)
    pre_gate = acc[:FB]
    pre_lin = acc[FB : 2 * FB]
    grad_act = acc[2 * FB :]
    gelu_value, gelu_slope = gelu_parts(pre_gate)
    gate = grad_act * pre_lin * gelu_slope
    lin = grad_act * gelu_value
    hidden_t[:FB] = gate.astype(jnp.bfloat16)
    hidden_t[FB : 2 * FB] = lin.astype(jnp.bfloat16)
    hidden_t[2 * FB :] = (gelu_value * pre_lin).astype(jnp.bfloat16)

    def backward(k, carry):
        w[k, : 2 * FB] = jnp.dot(
            hidden_t[: 2 * FB], x[0, k].reshape(TOK, DB), preferred_element_type=jnp.float32
        ).astype(jnp.bfloat16)
        w[k, 2 * FB :] = jnp.dot(
            hidden_t[2 * FB :], x[1, k].reshape(TOK, DB), preferred_element_type=jnp.float32
        ).astype(jnp.bfloat16)
        store(k).start()
        return carry

    lax.fori_loop(0, NZ, backward, 0)
    hidden[...] = hidden_t[: 2 * FB].T

    def finish(k, carry):
        store(k).wait()
        return carry

    lax.fori_loop(0, NZ, finish, 0)


def token_grad_kernel(place, hidden, weight, grad):
    for k in range(2):
        product = jnp.dot(hidden[...], weight[k], preferred_element_type=jnp.float32)
        product = product.astype(jnp.bfloat16).reshape(2, NY, NX, SUB, DB)
        for y in range(NY):
            for x in range(NX):
                for core in range(2):
                    grad[core, place[y * NX + x], k] = product[core, y, x]


def products(blocks, weight):
    hbm = pl.BlockSpec(memory_space=pltpu.HBM)
    return pl.pallas_call(
        main_kernel,
        in_specs=[pl.BlockSpec(memory_space=pl.ANY)] * 4 + [hbm],
        out_specs=[hbm, pl.BlockSpec(memory_space=pltpu.VMEM)],
        scratch_shapes=[
            pltpu.VMEM((2, NZ, 2, NY, NX, SUB, DB), jnp.bfloat16),
            pltpu.VMEM((NZ, 3 * FB, DB), jnp.bfloat16),
            pltpu.VMEM((3 * FB, TOK), jnp.float32),
            pltpu.VMEM((3 * FB, TOK), jnp.bfloat16),
            pltpu.SemaphoreType.DMA((NZ, 5)),
            pltpu.SemaphoreType.DMA((NZ,)),
        ],
        out_shape=[
            jax.ShapeDtypeStruct((NZ, 3 * FB, DB), jnp.bfloat16),
            jax.ShapeDtypeStruct((TOK, 2 * FB), jnp.bfloat16),
        ],
        compiler_params=pltpu.CompilerParams(vmem_limit_bytes=VMEM),
        cost_estimate=pl.CostEstimate(
            flops=4 * 3 * FB * TOK * D, bytes_accessed=25000000, transcendentals=FB * TOK
        ),
    )(*blocks, weight)


def token_grad(place, hidden, weight):
    return pl.pallas_call(
        token_grad_kernel,
        grid_spec=pltpu.PrefetchScalarGridSpec(
            num_scalar_prefetch=1,
            grid=(NZ // 2,),
            in_specs=[
                pl.BlockSpec((TOK, 2 * FB), lambda i, p: (0, 0)),
                pl.BlockSpec((2, 2 * FB, DB), lambda i, p: (i, 0, 0)),
            ],
            out_specs=pl.BlockSpec((2, NX * NY, 2, SUB, DB), lambda i, p: (0, 0, i, 0, 0)),
        ),
        out_shape=jax.ShapeDtypeStruct((2, NX * NY, NZ, SUB, DB), jnp.bfloat16),
        compiler_params=pltpu.CompilerParams(vmem_limit_bytes=VMEM),
        cost_estimate=pl.CostEstimate(
            flops=2 * 2 * FB * TOK * D, bytes_accessed=10000000, transcendentals=0
        ),
    )(place, hidden, weight)


def local(
    tokens,
    cotangent,
    wi_gate,
    wi_lin,
    wo,
    rows_gate,
    cols_gate,
    rows_lin,
    cols_lin,
    rows_out,
    cols_out,
    rate,
):
    bf16 = jnp.bfloat16
    weight = lax.all_gather(jnp.concatenate([wi_gate.T, wi_lin.T, wo], 0), "z", axis=0)

    pair = jnp.stack([tokens.reshape(NZ, SUB, DB), cotangent.reshape(NZ, SUB, DB)], 1)
    pair = lax.all_to_all(pair, "z", 0, 0, tiled=True)
    tok = gather4(gather4(pair[:, 0], "x", 0, 0), "y", 1, 0)
    cot = gather4(gather4(pair[:, 1], "y", 0, 0), "x", 1, 1)
    blocks = [tok, swap(tok), cot, swap(cot)]

    grad_w, hidden = products(blocks, weight)
    grad_w = lax.psum_scatter(grad_w, "z", scatter_dimension=0)

    shift = jnp.arange(4, dtype=jnp.int32)
    x_of = (lax.axis_index("x") + shift) % NX
    y_of = (lax.axis_index("y") + shift) % NY
    place = (x_of[None, :] * NY + y_of[:, None]).astype(jnp.int32).reshape(NX * NY)
    part = token_grad(place, hidden, weight)
    part = (part[0].astype(jnp.float32) + swap(part[1]).astype(jnp.float32)).astype(bf16)
    part = lax.all_to_all(part, ("x", "y"), 0, 0, tiled=True)
    part = jnp.sum(part.astype(jnp.float32), 0).astype(bf16)
    grad_tokens = lax.all_to_all(part, "z", 0, 0, tiled=True).reshape(tokens.shape)
    grad_w, grad_tokens = lax.optimization_barrier((grad_w, grad_tokens))

    grad = grad_w.astype(jnp.float32) * (1.0 / math.sqrt(4096.0))
    keep = 1.0 - decay_rate
    squares = grad * grad + 1e-30
    over_model = sum_over(jnp.sum(squares, 1), "z", NZ)
    hidden_old = jnp.concatenate([cols_gate, cols_lin, rows_out])
    hidden_new = decay_rate * hidden_old + keep * over_model / D
    model_old = jnp.stack([rows_gate, rows_lin, cols_out], 0)
    weighted = grad * grad / hidden_new[:, None]
    over_hidden = sum_col(
        jnp.concatenate(
            [
                jnp.sum(squares.reshape(3, FB, DB), 1),
                jnp.sum(weighted.reshape(3, FB, DB), 1),
            ],
            0,
        )
    )
    model_new = decay_rate * model_old + keep * over_hidden[:3] / FF
    totals = sum_over(jnp.sum(over_hidden[3:] / model_new, 1, keepdims=True), "z", NZ)
    factor = -rate[0] / jnp.sqrt(totals / (D * FF) + 1e-06)
    update = (
        grad.reshape(3, FB, DB)
        * lax.rsqrt(hidden_new).reshape(3, FB, 1)
        * (factor * lax.rsqrt(model_new)).reshape(3, 1, DB)
    )
    return (
        grad_tokens,
        update[0].T,
        update[1].T,
        update[2],
        model_new[0],
        hidden_new[:FB],
        model_new[1],
        hidden_new[FB : 2 * FB],
        hidden_new[2 * FB :],
        model_new[2],
    )


def solution(mesh):
    fine = Mesh(mesh.devices.reshape(NZ, NX, NY, NC), ("z",) + COL)
    return jax.shard_map(
        local,
        mesh=fine,
        in_specs=(
            P(None, COL, "z"),
            P(None, COL, "z"),
            P("z", COL),
            P("z", COL),
            P(COL, "z"),
            P("z"),
            P(COL),
            P("z"),
            P(COL),
            P(COL),
            P("z"),
            P(),
        ),
        out_specs=(
            P(None, COL, "z"),
            P("z", COL),
            P("z", COL),
            P(COL, "z"),
            P("z"),
            P(COL),
            P("z"),
            P(COL),
            P(COL),
            P("z"),
        ),
        check_vma=False,
    )
```

```python
import math

import jax
import jax.numpy as jnp
from jax import lax
from jax.experimental import pallas as pl
from jax.experimental.pallas import tpu as pltpu
from jax.sharding import Mesh
from jax.sharding import PartitionSpec as P

D = 4096
FF = 10240
NZ, NX, NY, NC = 8, 4, 4, 2
TOK = 512
SUB = 16
DB = D // NZ
FB = FF // (NX * NY * NC)

decay_rate = 0.8
gelu_coeff = math.sqrt(2.0 / math.pi)
COL = ("x", "y", "c")
SCALE = 1.0 / math.sqrt(4096.0)
VMEM = 48 * 1024 * 1024


def shifted(value, axis, step):
    return lax.ppermute(value, axis, [((i + step) % 4, i) for i in range(4)])


def swap(value):
    return lax.ppermute(value, "c", [(0, 1), (1, 0)])


def gather4(value, axis, model_dim, new_dim):
    right = shifted(value, axis, 1)
    left = shifted(value, axis, 3)
    low = lax.slice_in_dim(right, 0, NZ // 2, axis=model_dim)
    high = lax.slice_in_dim(left, NZ // 2, NZ, axis=model_dim)
    far = jnp.concatenate([shifted(low, axis, 1), shifted(high, axis, 3)], model_dim)
    return jnp.stack([value, right, far, left], new_dim)


def sum_over(value, axis, size):
    copies = jnp.broadcast_to(value[None], (size,) + value.shape)
    return jnp.sum(lax.all_to_all(copies, axis, 0, 0, tiled=True), 0)


def sum_col(value):
    return sum_over(value + swap(value), ("x", "y"), NX * NY)


def gelu_parts(value):
    inner = gelu_coeff * (value + 0.044715 * value * value * value)
    tangent = jnp.tanh(inner)
    gelu_value = 0.5 * value * (1.0 + tangent)
    gelu_slope = 0.5 * (1.0 + tangent) + 0.5 * value * (1.0 - tangent * tangent) * gelu_coeff * (
        1.0 + 3.0 * 0.044715 * value * value
    )
    return (gelu_value, gelu_slope)


def dot_nt(left, right):
    return lax.dot_general(
        left, right, (((1,), (1,)), ((), ())), preferred_element_type=jnp.float32
    )


def main_kernel(tok0, tok1, cot0, cot1, weight, grad, hidden, x, w, acc, hidden_t, sems, out_sems):
    def loads(k):
        sources = (tok0, tok1, cot0, cot1)
        copies = [
            pltpu.make_async_copy(source.at[:, :, k], x.at[m // 2, k, m % 2], sems.at[k, m])
            for m, source in enumerate(sources)
        ]
        return copies + [pltpu.make_async_copy(weight.at[k], w.at[k], sems.at[k, 4])]

    def store(k):
        return pltpu.make_async_copy(w.at[k], grad.at[k], out_sems.at[k])

    def start(k, carry):
        for copy in loads(k):
            copy.start()
        return carry

    lax.fori_loop(0, NZ, start, 0)
    acc[...] = jnp.zeros_like(acc)

    def forward(pair, carry):
        first = second = 0.0
        for k in (2 * pair, 2 * pair + 1):
            for copy in loads(k):
                copy.wait()
            first += dot_nt(w[k, : 2 * FB], x[0, k].reshape(TOK, DB))
            second += dot_nt(w[k, 2 * FB :], x[1, k].reshape(TOK, DB))
        acc[: 2 * FB] += first
        acc[2 * FB :] += second
        return carry

    lax.fori_loop(0, NZ // 2, forward, 0)
    pre_gate = acc[:FB]
    pre_lin = acc[FB : 2 * FB]
    grad_act = acc[2 * FB :]
    gelu_value, gelu_slope = gelu_parts(pre_gate)
    gate = grad_act * pre_lin * gelu_slope
    lin = grad_act * gelu_value
    hidden_t[:FB] = gate.astype(jnp.bfloat16)
    hidden_t[FB : 2 * FB] = lin.astype(jnp.bfloat16)
    hidden_t[2 * FB :] = (gelu_value * pre_lin).astype(jnp.bfloat16)

    def backward(k, carry):
        w[k, : 2 * FB] = jnp.dot(
            hidden_t[: 2 * FB], x[0, k].reshape(TOK, DB), preferred_element_type=jnp.float32
        ).astype(jnp.bfloat16)
        w[k, 2 * FB :] = jnp.dot(
            hidden_t[2 * FB :], x[1, k].reshape(TOK, DB), preferred_element_type=jnp.float32
        ).astype(jnp.bfloat16)
        store(k).start()
        return carry

    lax.fori_loop(0, NZ, backward, 0)
    hidden[...] = hidden_t[: 2 * FB].T

    def finish(k, carry):
        store(k).wait()
        return carry

    lax.fori_loop(0, NZ, finish, 0)


def token_grad_kernel(place, hidden, weight, grad):
    for k in range(2):
        product = jnp.dot(hidden[...], weight[k], preferred_element_type=jnp.float32)
        product = product.astype(jnp.bfloat16).reshape(2, NY, NX, SUB, DB)
        for y in range(NY):
            for x in range(NX):
                for core in range(2):
                    grad[core, place[y * NX + x], k] = product[core, y, x]


def products(blocks, weight):
    hbm = pl.BlockSpec(memory_space=pltpu.HBM)
    return pl.pallas_call(
        main_kernel,
        in_specs=[pl.BlockSpec(memory_space=pl.ANY)] * 4 + [hbm],
        out_specs=[hbm, pl.BlockSpec(memory_space=pltpu.VMEM)],
        scratch_shapes=[
            pltpu.VMEM((2, NZ, 2, NY, NX, SUB, DB), jnp.bfloat16),
            pltpu.VMEM((NZ, 3 * FB, DB), jnp.bfloat16),
            pltpu.VMEM((3 * FB, TOK), jnp.float32),
            pltpu.VMEM((3 * FB, TOK), jnp.bfloat16),
            pltpu.SemaphoreType.DMA((NZ, 5)),
            pltpu.SemaphoreType.DMA((NZ,)),
        ],
        out_shape=[
            jax.ShapeDtypeStruct((NZ, 3 * FB, DB), jnp.bfloat16),
            jax.ShapeDtypeStruct((TOK, 2 * FB), jnp.bfloat16),
        ],
        compiler_params=pltpu.CompilerParams(vmem_limit_bytes=VMEM),
        cost_estimate=pl.CostEstimate(
            flops=4 * 3 * FB * TOK * D, bytes_accessed=25000000, transcendentals=FB * TOK
        ),
    )(*blocks, weight)


def token_grad(place, hidden, weight):
    return pl.pallas_call(
        token_grad_kernel,
        grid_spec=pltpu.PrefetchScalarGridSpec(
            num_scalar_prefetch=1,
            grid=(NZ // 2,),
            in_specs=[
                pl.BlockSpec((TOK, 2 * FB), lambda i, p: (0, 0)),
                pl.BlockSpec((2, 2 * FB, DB), lambda i, p: (i, 0, 0)),
            ],
            out_specs=pl.BlockSpec((2, NX * NY, 2, SUB, DB), lambda i, p: (0, 0, i, 0, 0)),
        ),
        out_shape=jax.ShapeDtypeStruct((2, NX * NY, NZ, SUB, DB), jnp.bfloat16),
        compiler_params=pltpu.CompilerParams(vmem_limit_bytes=VMEM),
        cost_estimate=pl.CostEstimate(
            flops=2 * 2 * FB * TOK * D, bytes_accessed=10000000, transcendentals=0
        ),
    )(place, hidden, weight)


def settle_kernel(value, result):
    result[...] = value[...]


def settle(value):
    return pl.pallas_call(
        settle_kernel, out_shape=jax.ShapeDtypeStruct(value.shape, value.dtype)
    )(value)


def local(
    tokens,
    cotangent,
    wi_gate,
    wi_lin,
    wo,
    rows_gate,
    cols_gate,
    rows_lin,
    cols_lin,
    rows_out,
    cols_out,
    rate,
):
    bf16 = jnp.bfloat16
    weight = lax.all_gather(jnp.concatenate([wi_gate.T, wi_lin.T, wo], 0), "z", axis=0)

    pair = jnp.stack([tokens.reshape(NZ, SUB, DB), cotangent.reshape(NZ, SUB, DB)], 1)
    pair = lax.all_to_all(pair, "z", 0, 0, tiled=True)
    tok = gather4(gather4(pair[:, 0], "x", 0, 0), "y", 1, 0)
    cot = gather4(gather4(pair[:, 1], "y", 0, 0), "x", 1, 1)
    blocks = [tok, swap(tok), cot, swap(cot)]

    grad_w, hidden = products(blocks, weight)
    grad_w = lax.psum_scatter(grad_w, "z", scatter_dimension=0)

    shift = jnp.arange(4, dtype=jnp.int32)
    x_of = (lax.axis_index("x") + shift) % NX
    y_of = (lax.axis_index("y") + shift) % NY
    place = (x_of[None, :] * NY + y_of[:, None]).astype(jnp.int32).reshape(NX * NY)
    part = token_grad(place, hidden, weight)
    part = (part[0].astype(jnp.float32) + swap(part[1]).astype(jnp.float32)).astype(bf16)
    part = lax.all_to_all(part, ("x", "y"), 0, 0, tiled=True)
    part = jnp.sum(part.astype(jnp.float32), 0).astype(bf16)
    grad_tokens = settle(lax.all_to_all(part, "z", 0, 0, tiled=True).reshape(tokens.shape))
    grad_w, grad_tokens = lax.optimization_barrier((grad_w, grad_tokens))

    keep = 1.0 - decay_rate
    first = grad_w.astype(jnp.float32) * SCALE
    first = jnp.sum(first * first + 1e-30, 1)
    first, grad_w = lax.optimization_barrier((first, grad_w))
    grad = lax.optimization_barrier(grad_w.reshape(3, FB, DB).astype(jnp.float32) * SCALE)
    over_model = sum_over(first, "z", NZ).reshape(3, FB)
    plain = jnp.sum(grad * grad + 1e-30, 1)
    hidden_old = jnp.stack([cols_gate, cols_lin, rows_out], 0)
    hidden_new = decay_rate * hidden_old + keep * over_model / D
    model_old = jnp.stack([rows_gate, rows_lin, cols_out], 0)
    weighted = jnp.sum(grad * grad * (1.0 / hidden_new).reshape(3, FB, 1), 1)
    over_hidden = sum_col(jnp.concatenate([plain, weighted], 0))
    model_new = decay_rate * model_old + keep * over_hidden[:3] / FF
    totals = sum_over(jnp.sum(over_hidden[3:] / model_new, 1, keepdims=True), "z", NZ)
    factor = -rate[0] / jnp.sqrt(totals / (D * FF) + 1e-06)
    update = (
        grad
        * lax.rsqrt(hidden_new).reshape(3, FB, 1)
        * (factor * lax.rsqrt(model_new)).reshape(3, 1, DB)
    )
    return (
        grad_tokens,
        update[0].T,
        update[1].T,
        update[2],
        model_new[0],
        hidden_new[0],
        model_new[1],
        hidden_new[1],
        hidden_new[2],
        model_new[2],
    )


def solution(mesh):
    fine = Mesh(mesh.devices.reshape(NZ, NX, NY, NC), ("z",) + COL)
    return jax.shard_map(
        local,
        mesh=fine,
        in_specs=(
            P(None, COL, "z"),
            P(None, COL, "z"),
            P("z", COL),
            P("z", COL),
            P(COL, "z"),
            P("z"),
            P(COL),
            P("z"),
            P(COL),
            P(COL),
            P("z"),
            P(),
        ),
        out_specs=(
            P(None, COL, "z"),
            P("z", COL),
            P("z", COL),
            P(COL, "z"),
            P("z"),
            P(COL),
            P("z"),
            P(COL),
            P(COL),
            P("z"),
        ),
        check_vma=False,
    )
```

```python
import math

import jax
import jax.numpy as jnp
from jax import lax
from jax.experimental import pallas as pl
from jax.experimental.pallas import tpu as pltpu
from jax.sharding import Mesh
from jax.sharding import PartitionSpec as P

D = 4096
FF = 10240
NZ, NX, NY, NC = 8, 4, 4, 2
TOK = 512
SUB = 16
DB = D // NZ
FB = FF // (NX * NY * NC)

decay_rate = 0.8
gelu_coeff = math.sqrt(2.0 / math.pi)
COL = ("x", "y", "c")
SCALE = 1.0 / math.sqrt(4096.0)
VMEM = 48 * 1024 * 1024


def shifted(value, axis, step):
    return lax.ppermute(value, axis, [((i + step) % 4, i) for i in range(4)])


def swap(value):
    return lax.ppermute(value, "c", [(0, 1), (1, 0)])


def gather4(value, axis, model_dim, new_dim):
    right = shifted(value, axis, 1)
    left = shifted(value, axis, 3)
    low = lax.slice_in_dim(right, 0, NZ // 2, axis=model_dim)
    high = lax.slice_in_dim(left, NZ // 2, NZ, axis=model_dim)
    far = jnp.concatenate([shifted(low, axis, 1), shifted(high, axis, 3)], model_dim)
    return jnp.stack([value, right, far, left], new_dim)


def sum_over(value, axis, size):
    copies = jnp.broadcast_to(value[None], (size,) + value.shape)
    return jnp.sum(lax.all_to_all(copies, axis, 0, 0, tiled=True), 0)


def sum_col(value):
    return sum_over(value + swap(value), ("x", "y"), NX * NY)


def gelu_parts(value):
    inner = gelu_coeff * (value + 0.044715 * value * value * value)
    tangent = jnp.tanh(inner)
    gelu_value = 0.5 * value * (1.0 + tangent)
    gelu_slope = 0.5 * (1.0 + tangent) + 0.5 * value * (1.0 - tangent * tangent) * gelu_coeff * (
        1.0 + 3.0 * 0.044715 * value * value
    )
    return (gelu_value, gelu_slope)


def dot_nt(left, right):
    return lax.dot_general(
        left, right, (((1,), (1,)), ((), ())), preferred_element_type=jnp.float32
    )


def main_kernel(tok0, tok1, cot0, cot1, weight, grad, hidden, x, w, acc, hidden_t, sems, out_sems):
    def loads(k):
        sources = (tok0, tok1, cot0, cot1)
        copies = [
            pltpu.make_async_copy(source.at[:, :, k], x.at[m // 2, k, m % 2], sems.at[k, m])
            for m, source in enumerate(sources)
        ]
        return copies + [pltpu.make_async_copy(weight.at[k], w.at[k], sems.at[k, 4])]

    def store(k):
        return pltpu.make_async_copy(w.at[k], grad.at[k], out_sems.at[k])

    def start(k, carry):
        for copy in loads(k):
            copy.start()
        return carry

    lax.fori_loop(0, NZ, start, 0)
    acc[...] = jnp.zeros_like(acc)

    def forward(pair, carry):
        first = second = 0.0
        for k in (2 * pair, 2 * pair + 1):
            for copy in loads(k):
                copy.wait()
            first += dot_nt(w[k, : 2 * FB], x[0, k].reshape(TOK, DB))
            second += dot_nt(w[k, 2 * FB :], x[1, k].reshape(TOK, DB))
        acc[: 2 * FB] += first
        acc[2 * FB :] += second
        return carry

    for pair in range(NZ // 2):
        forward(pair, 0)
    pre_gate = acc[:FB]
    pre_lin = acc[FB : 2 * FB]
    grad_act = acc[2 * FB :]
    gelu_value, gelu_slope = gelu_parts(pre_gate)
    gate = grad_act * pre_lin * gelu_slope
    lin = grad_act * gelu_value
    hidden_t[:FB] = gate.astype(jnp.bfloat16)
    hidden_t[FB : 2 * FB] = lin.astype(jnp.bfloat16)
    hidden_t[2 * FB :] = (gelu_value * pre_lin).astype(jnp.bfloat16)

    def backward(k, carry):
        w[k, : 2 * FB] = jnp.dot(
            hidden_t[: 2 * FB], x[0, k].reshape(TOK, DB), preferred_element_type=jnp.float32
        ).astype(jnp.bfloat16)
        w[k, 2 * FB :] = jnp.dot(
            hidden_t[2 * FB :], x[1, k].reshape(TOK, DB), preferred_element_type=jnp.float32
        ).astype(jnp.bfloat16)
        store(k).start()
        return carry

    for k in range(NZ):
        backward(k, 0)
    hidden[...] = hidden_t[: 2 * FB].T

    def finish(k, carry):
        store(k).wait()
        return carry

    lax.fori_loop(0, NZ, finish, 0)


def token_grad_kernel(place, hidden, weight, grad):
    for k in range(2):
        product = jnp.dot(hidden[...], weight[k], preferred_element_type=jnp.float32)
        product = product.astype(jnp.bfloat16).reshape(2, NY, NX, SUB, DB)
        for y in range(NY):
            for x in range(NX):
                for core in range(2):
                    grad[core, place[y * NX + x], k] = product[core, y, x]


def products(blocks, weight):
    hbm = pl.BlockSpec(memory_space=pltpu.HBM)
    return pl.pallas_call(
        main_kernel,
        in_specs=[pl.BlockSpec(memory_space=pl.ANY)] * 4 + [hbm],
        out_specs=[hbm, pl.BlockSpec(memory_space=pltpu.VMEM)],
        scratch_shapes=[
            pltpu.VMEM((2, NZ, 2, NY, NX, SUB, DB), jnp.bfloat16),
            pltpu.VMEM((NZ, 3 * FB, DB), jnp.bfloat16),
            pltpu.VMEM((3 * FB, TOK), jnp.float32),
            pltpu.VMEM((3 * FB, TOK), jnp.bfloat16),
            pltpu.SemaphoreType.DMA((NZ, 5)),
            pltpu.SemaphoreType.DMA((NZ,)),
        ],
        out_shape=[
            jax.ShapeDtypeStruct((NZ, 3 * FB, DB), jnp.bfloat16),
            jax.ShapeDtypeStruct((TOK, 2 * FB), jnp.bfloat16),
        ],
        compiler_params=pltpu.CompilerParams(vmem_limit_bytes=60 * 1024 * 1024),
        cost_estimate=pl.CostEstimate(
            flops=4 * 3 * FB * TOK * D, bytes_accessed=25000000, transcendentals=FB * TOK
        ),
    )(*blocks, weight)


def token_grad(place, hidden, weight):
    return pl.pallas_call(
        token_grad_kernel,
        grid_spec=pltpu.PrefetchScalarGridSpec(
            num_scalar_prefetch=1,
            grid=(NZ // 2,),
            in_specs=[
                pl.BlockSpec((TOK, 2 * FB), lambda i, p: (0, 0)),
                pl.BlockSpec((2, 2 * FB, DB), lambda i, p: (i, 0, 0)),
            ],
            out_specs=pl.BlockSpec((2, NX * NY, 2, SUB, DB), lambda i, p: (0, 0, i, 0, 0)),
        ),
        out_shape=jax.ShapeDtypeStruct((2, NX * NY, NZ, SUB, DB), jnp.bfloat16),
        compiler_params=pltpu.CompilerParams(vmem_limit_bytes=VMEM),
        cost_estimate=pl.CostEstimate(
            flops=2 * 2 * FB * TOK * D, bytes_accessed=10000000, transcendentals=0
        ),
    )(place, hidden, weight)


def settle_kernel(value, result):
    result[...] = value[...]


def settle(value):
    return pl.pallas_call(
        settle_kernel, out_shape=jax.ShapeDtypeStruct(value.shape, value.dtype)
    )(value)


def local(
    tokens,
    cotangent,
    wi_gate,
    wi_lin,
    wo,
    rows_gate,
    cols_gate,
    rows_lin,
    cols_lin,
    rows_out,
    cols_out,
    rate,
):
    bf16 = jnp.bfloat16
    weight = lax.all_gather(jnp.concatenate([wi_gate.T, wi_lin.T, wo], 0), "z", axis=0)

    pair = jnp.stack([tokens.reshape(NZ, SUB, DB), cotangent.reshape(NZ, SUB, DB)], 1)
    pair = lax.all_to_all(pair, "z", 0, 0, tiled=True)
    tok = gather4(gather4(pair[:, 0], "x", 0, 0), "y", 1, 0)
    cot = gather4(gather4(pair[:, 1], "y", 0, 0), "x", 1, 1)
    blocks = [tok, swap(tok), cot, swap(cot)]

    grad_w, hidden = products(blocks, weight)
    grad_w = lax.psum_scatter(grad_w, "z", scatter_dimension=0)

    shift = jnp.arange(4, dtype=jnp.int32)
    x_of = (lax.axis_index("x") + shift) % NX
    y_of = (lax.axis_index("y") + shift) % NY
    place = (x_of[None, :] * NY + y_of[:, None]).astype(jnp.int32).reshape(NX * NY)
    part = token_grad(place, hidden, weight)
    part = (part[0].astype(jnp.float32) + swap(part[1]).astype(jnp.float32)).astype(bf16)
    part = lax.all_to_all(part, ("x", "y"), 0, 0, tiled=True)
    part = jnp.sum(part.astype(jnp.float32), 0).astype(bf16)
    grad_tokens = settle(lax.all_to_all(part, "z", 0, 0, tiled=True).reshape(tokens.shape))
    grad_w, grad_tokens = lax.optimization_barrier((grad_w, grad_tokens))

    keep = 1.0 - decay_rate
    first = grad_w.astype(jnp.float32) * SCALE
    first = jnp.sum(first * first + 1e-30, 1)
    first, grad_w = lax.optimization_barrier((first, grad_w))
    grad = lax.optimization_barrier(grad_w.reshape(3, FB, DB).astype(jnp.float32) * SCALE)
    over_model = sum_over(first, "z", NZ).reshape(3, FB)
    plain = jnp.sum(grad * grad + 1e-30, 1)
    hidden_old = jnp.stack([cols_gate, cols_lin, rows_out], 0)
    hidden_new = decay_rate * hidden_old + keep * over_model / D
    model_old = jnp.stack([rows_gate, rows_lin, cols_out], 0)
    weighted = jnp.sum(grad * grad * (1.0 / hidden_new).reshape(3, FB, 1), 1)
    over_hidden = sum_col(jnp.concatenate([plain, weighted], 0))
    model_new = decay_rate * model_old + keep * over_hidden[:3] / FF
    totals = sum_over(jnp.sum(over_hidden[3:] / model_new, 1, keepdims=True), "z", NZ)
    factor = -rate[0] / jnp.sqrt(totals / (D * FF) + 1e-06)
    update = (
        grad
        * lax.rsqrt(hidden_new).reshape(3, FB, 1)
        * (factor * lax.rsqrt(model_new)).reshape(3, 1, DB)
    )
    return (
        grad_tokens,
        update[0].T,
        update[1].T,
        update[2],
        model_new[0],
        hidden_new[0],
        model_new[1],
        hidden_new[1],
        hidden_new[2],
        model_new[2],
    )


def solution(mesh):
    fine = Mesh(mesh.devices.reshape(NZ, NX, NY, NC), ("z",) + COL)
    return jax.shard_map(
        local,
        mesh=fine,
        in_specs=(
            P(None, COL, "z"),
            P(None, COL, "z"),
            P("z", COL),
            P("z", COL),
            P(COL, "z"),
            P("z"),
            P(COL),
            P("z"),
            P(COL),
            P(COL),
            P("z"),
            P(),
        ),
        out_specs=(
            P(None, COL, "z"),
            P("z", COL),
            P("z", COL),
            P(COL, "z"),
            P("z"),
            P(COL),
            P("z"),
            P(COL),
            P(COL),
            P("z"),
        ),
        check_vma=False,
    )
```

```python
import math

import jax
import jax.numpy as jnp
from jax import lax
from jax.experimental import pallas as pl
from jax.experimental.pallas import tpu as pltpu
from jax.sharding import Mesh
from jax.sharding import PartitionSpec as P

D = 4096
FF = 10240
NZ, NX, NY, NC = 8, 4, 4, 2
TOK = 512
SUB = 16
DB = D // NZ
FB = FF // (NX * NY * NC)

decay_rate = 0.8
gelu_coeff = math.sqrt(2.0 / math.pi)
COL = ("x", "y", "c")
SCALE = 1.0 / math.sqrt(4096.0)
VMEM = 48 * 1024 * 1024


def shifted(value, axis, step):
    return lax.ppermute(value, axis, [((i + step) % 4, i) for i in range(4)])


def swap(value):
    return lax.ppermute(value, "c", [(0, 1), (1, 0)])


def gather4(value, axis, model_dim, new_dim):
    right = shifted(value, axis, 1)
    left = shifted(value, axis, 3)
    low = lax.slice_in_dim(right, 0, NZ // 2, axis=model_dim)
    high = lax.slice_in_dim(left, NZ // 2, NZ, axis=model_dim)
    far = jnp.concatenate([shifted(low, axis, 1), shifted(high, axis, 3)], model_dim)
    return jnp.stack([value, right, far, left], new_dim)


def sum_over(value, axis, size):
    copies = jnp.broadcast_to(value[None], (size,) + value.shape)
    return jnp.sum(lax.all_to_all(copies, axis, 0, 0, tiled=True), 0)


def sum_col(value):
    return sum_over(value + swap(value), ("x", "y"), NX * NY)


def gelu_parts(value):
    inner = gelu_coeff * (value + 0.044715 * value * value * value)
    tangent = jnp.tanh(inner)
    gelu_value = 0.5 * value * (1.0 + tangent)
    gelu_slope = 0.5 * (1.0 + tangent) + 0.5 * value * (1.0 - tangent * tangent) * gelu_coeff * (
        1.0 + 3.0 * 0.044715 * value * value
    )
    return (gelu_value, gelu_slope)


def dot_nt(left, right):
    return lax.dot_general(
        left, right, (((1,), (1,)), ((), ())), preferred_element_type=jnp.float32
    )


def main_kernel(tok0, tok1, cot0, cot1, weight, grad, hidden, x, w, acc, hidden_t, sems, out_sems):
    def loads(k):
        sources = (tok0, tok1, cot0, cot1)
        copies = [
            pltpu.make_async_copy(source.at[:, :, k], x.at[m // 2, k, m % 2], sems.at[k, m])
            for m, source in enumerate(sources)
        ]
        return copies + [pltpu.make_async_copy(weight.at[k], w.at[k], sems.at[k, 4])]

    def store(k):
        return pltpu.make_async_copy(w.at[k], grad.at[k], out_sems.at[k])

    def start(k, carry):
        for copy in loads(k):
            copy.start()
        return carry

    lax.fori_loop(0, NZ, start, 0)

    def forward(pair, carry):
        first = second = 0.0
        for k in (2 * pair, 2 * pair + 1):
            for copy in loads(k):
                copy.wait()
            first += dot_nt(w[k, : 2 * FB], x[0, k].reshape(TOK, DB))
            second += dot_nt(w[k, 2 * FB :], x[1, k].reshape(TOK, DB))
        acc[: 2 * FB] = first if pair == 0 else acc[: 2 * FB] + first
        acc[2 * FB :] = second if pair == 0 else acc[2 * FB :] + second
        return carry

    for pair in range(NZ // 2):
        forward(pair, 0)
    pre_gate = acc[:FB]
    pre_lin = acc[FB : 2 * FB]
    grad_act = acc[2 * FB :]
    gelu_value, gelu_slope = gelu_parts(pre_gate)
    gate = grad_act * pre_lin * gelu_slope
    lin = grad_act * gelu_value
    hidden_t[:FB] = gate.astype(jnp.bfloat16)
    hidden_t[FB : 2 * FB] = lin.astype(jnp.bfloat16)
    hidden_t[2 * FB :] = (gelu_value * pre_lin).astype(jnp.bfloat16)

    def backward(k, carry):
        w[k, : 2 * FB] = jnp.dot(
            hidden_t[: 2 * FB], x[0, k].reshape(TOK, DB), preferred_element_type=jnp.float32
        ).astype(jnp.bfloat16)
        w[k, 2 * FB :] = jnp.dot(
            hidden_t[2 * FB :], x[1, k].reshape(TOK, DB), preferred_element_type=jnp.float32
        ).astype(jnp.bfloat16)
        store(k).start()
        return carry

    for k in range(NZ):
        backward(k, 0)
    hidden[...] = hidden_t[: 2 * FB].T

    def finish(k, carry):
        store(k).wait()
        return carry

    lax.fori_loop(0, NZ, finish, 0)


def token_grad_kernel(place, hidden, weight, grad):
    for k in range(2):
        product = jnp.dot(hidden[...], weight[k], preferred_element_type=jnp.float32)
        product = product.astype(jnp.bfloat16).reshape(2, NY, NX, SUB, DB)
        for y in range(NY):
            for x in range(NX):
                for core in range(2):
                    grad[core, place[y * NX + x], k] = product[core, y, x]


def products(blocks, weight):
    hbm = pl.BlockSpec(memory_space=pltpu.HBM)
    return pl.pallas_call(
        main_kernel,
        in_specs=[pl.BlockSpec(memory_space=pl.ANY)] * 4 + [hbm],
        out_specs=[hbm, pl.BlockSpec(memory_space=pltpu.VMEM)],
        scratch_shapes=[
            pltpu.VMEM((2, NZ, 2, NY, NX, SUB, DB), jnp.bfloat16),
            pltpu.VMEM((NZ, 3 * FB, DB), jnp.bfloat16),
            pltpu.VMEM((3 * FB, TOK), jnp.float32),
            pltpu.VMEM((3 * FB, TOK), jnp.bfloat16),
            pltpu.SemaphoreType.DMA((NZ, 5)),
            pltpu.SemaphoreType.DMA((NZ,)),
        ],
        out_shape=[
            jax.ShapeDtypeStruct((NZ, 3 * FB, DB), jnp.bfloat16),
            jax.ShapeDtypeStruct((TOK, 2 * FB), jnp.bfloat16),
        ],
        compiler_params=pltpu.CompilerParams(vmem_limit_bytes=60 * 1024 * 1024),
        cost_estimate=pl.CostEstimate(
            flops=4 * 3 * FB * TOK * D, bytes_accessed=25000000, transcendentals=FB * TOK
        ),
    )(*blocks, weight)


def token_grad(place, hidden, weight):
    return pl.pallas_call(
        token_grad_kernel,
        grid_spec=pltpu.PrefetchScalarGridSpec(
            num_scalar_prefetch=1,
            grid=(NZ // 2,),
            in_specs=[
                pl.BlockSpec((TOK, 2 * FB), lambda i, p: (0, 0)),
                pl.BlockSpec((2, 2 * FB, DB), lambda i, p: (i, 0, 0)),
            ],
            out_specs=pl.BlockSpec((2, NX * NY, 2, SUB, DB), lambda i, p: (0, 0, i, 0, 0)),
        ),
        out_shape=jax.ShapeDtypeStruct((2, NX * NY, NZ, SUB, DB), jnp.bfloat16),
        compiler_params=pltpu.CompilerParams(vmem_limit_bytes=VMEM),
        cost_estimate=pl.CostEstimate(
            flops=2 * 2 * FB * TOK * D, bytes_accessed=10000000, transcendentals=0
        ),
    )(place, hidden, weight)


def settle_kernel(value, result):
    result[...] = value[...]


def settle(value):
    return pl.pallas_call(
        settle_kernel, out_shape=jax.ShapeDtypeStruct(value.shape, value.dtype)
    )(value)


def local(
    tokens,
    cotangent,
    wi_gate,
    wi_lin,
    wo,
    rows_gate,
    cols_gate,
    rows_lin,
    cols_lin,
    rows_out,
    cols_out,
    rate,
):
    bf16 = jnp.bfloat16
    weight = lax.all_gather(jnp.concatenate([wi_gate.T, wi_lin.T, wo], 0), "z", axis=0)

    pair = jnp.stack([tokens.reshape(NZ, SUB, DB), cotangent.reshape(NZ, SUB, DB)], 1)
    pair = lax.all_to_all(pair, "z", 0, 0, tiled=True)
    tok = gather4(gather4(pair[:, 0], "x", 0, 0), "y", 1, 0)
    cot = gather4(gather4(pair[:, 1], "y", 0, 0), "x", 1, 1)
    blocks = [tok, swap(tok), cot, swap(cot)]

    grad_w, hidden = products(blocks, weight)
    grad_w = lax.psum_scatter(grad_w, "z", scatter_dimension=0)

    shift = jnp.arange(4, dtype=jnp.int32)
    x_of = (lax.axis_index("x") + shift) % NX
    y_of = (lax.axis_index("y") + shift) % NY
    place = (x_of[None, :] * NY + y_of[:, None]).astype(jnp.int32).reshape(NX * NY)
    part = token_grad(place, hidden, weight)
    part = (part[0].astype(jnp.float32) + swap(part[1]).astype(jnp.float32)).astype(bf16)
    part = lax.all_to_all(part, ("x", "y"), 0, 0, tiled=True)
    part = jnp.sum(part.astype(jnp.float32), 0).astype(bf16)
    grad_tokens = settle(lax.all_to_all(part, "z", 0, 0, tiled=True).reshape(tokens.shape))
    grad_w, grad_tokens = lax.optimization_barrier((grad_w, grad_tokens))

    keep = 1.0 - decay_rate
    first = grad_w.astype(jnp.float32) * SCALE
    first = jnp.sum(first * first + 1e-30, 1)
    first, grad_w = lax.optimization_barrier((first, grad_w))
    grad = lax.optimization_barrier(grad_w.reshape(3, FB, DB).astype(jnp.float32) * SCALE)
    over_model = sum_over(first, "z", NZ).reshape(3, FB)
    plain = jnp.sum(grad * grad + 1e-30, 1)
    hidden_old = jnp.stack([cols_gate, cols_lin, rows_out], 0)
    hidden_new = decay_rate * hidden_old + keep * over_model / D
    model_old = jnp.stack([rows_gate, rows_lin, cols_out], 0)
    weighted = jnp.sum(grad * grad * (1.0 / hidden_new).reshape(3, FB, 1), 1)
    over_hidden = sum_col(jnp.concatenate([plain, weighted], 0))
    model_new = decay_rate * model_old + keep * over_hidden[:3] / FF
    totals = sum_over(jnp.sum(over_hidden[3:] / model_new, 1, keepdims=True), "z", NZ)
    factor = -rate[0] / jnp.sqrt(totals / (D * FF) + 1e-06)
    update = (
        grad
        * lax.rsqrt(hidden_new).reshape(3, FB, 1)
        * (factor * lax.rsqrt(model_new)).reshape(3, 1, DB)
    )
    return (
        grad_tokens,
        update[0].T,
        update[1].T,
        update[2],
        model_new[0],
        hidden_new[0],
        model_new[1],
        hidden_new[1],
        hidden_new[2],
        model_new[2],
    )


def solution(mesh):
    fine = Mesh(mesh.devices.reshape(NZ, NX, NY, NC), ("z",) + COL)
    return jax.shard_map(
        local,
        mesh=fine,
        in_specs=(
            P(None, COL, "z"),
            P(None, COL, "z"),
            P("z", COL),
            P("z", COL),
            P(COL, "z"),
            P("z"),
            P(COL),
            P("z"),
            P(COL),
            P(COL),
            P("z"),
            P(),
        ),
        out_specs=(
            P(None, COL, "z"),
            P("z", COL),
            P("z", COL),
            P(COL, "z"),
            P("z"),
            P(COL),
            P("z"),
            P(COL),
            P(COL),
            P("z"),
        ),
        check_vma=False,
    )
```
